32 devices in a mesh: shard: 8 (over z, y), tensor: 4 (over x, core).
Axes of the slice: x: 2, y: 2, z: 4, core: 2. Of those that a mesh axis runs over, the one named last changes fastest.
Arguments:
- gradient: bfloat16 [8, 1024, 1024], P(None, 'shard', 'tensor'), may hold values from -64 to 64, as said below
- momentum: float32 [8, 1024, 1024], P(None, 'shard', 'tensor'), may hold values from -64 to 64, as said below
Outputs:
- momentum_out: float32 [8, 1024, 1024], P(None, 'shard', 'tensor')
- update: float32 [8, 1024, 1024], P(None, 'shard', 'tensor')
The draws below stay inside these ranges and needn't reach their ends.
Inputs may be any that keep to these rules, and one draw needn't show every extreme that they name: `gradient`: finite real values. `momentum`: finite real values.
All inputs are finite; a program needn't handle non-finite values.
Results may differ from the reference program's by a relative error of at most 0.0003.
Values sent between devices are 32-bit elements; how exact they have to be, the bound alone decides.
A program may use at most 64 MiB of HBM per device.

```python
import math
import jax
import jax.numpy as jnp
from jax import lax

D = 1024
BLOCK = 1024
ITERS = 3
NB = 8


def scaled_field(key):
    noise_key, rows_key, column_key = jax.random.split(key, 3)
    row_scale = jnp.exp(jax.random.uniform(rows_key, (NB, BLOCK, 1), jnp.float32, 0.0, math.log(10.0)))
    column_scale = jnp.exp(jax.random.uniform(column_key, (NB, 1, D), jnp.float32, 0.0, math.log(10.0)))
    field_values = jnp.clip(jax.random.normal(noise_key, (NB, BLOCK, D), jnp.float32), -6.0, 6.0)
    return field_values * row_scale * column_scale / 10.0


def draw_gradient(key, part):
    return scaled_field(key).astype(jnp.bfloat16)


def draw_momentum(key, part):
    return scaled_field(jax.random.fold_in(key, 7)).astype(jnp.float32)


def setup_inputs(seed: int = 0) -> dict:
    keys = jax.random.split(jax.random.key(seed), 3)
    return {
        "gradient": draw_gradient(jax.random.fold_in(keys[2], 71), 0),
        "momentum": draw_momentum(jax.random.fold_in(keys[2], 71), 0),
    }


first_coef = 3.4445
second_coef = -4.775
third_coef = 2.0315
decay_rate = 0.95

def orthogonalize(matrix):
    frobenius = jnp.sqrt(jnp.sum(matrix * matrix)) + 1e-07
    iterate = matrix / frobenius
    for sweep_index in range(ITERS):
        gram_matrix = jnp.einsum('ij,lj->il', iterate, iterate, precision=lax.Precision.HIGHEST, preferred_element_type=jnp.float32)
        square = jnp.einsum('ij,jl->il', gram_matrix, gram_matrix, precision=lax.Precision.HIGHEST, preferred_element_type=jnp.float32)
        polynomial = second_coef * gram_matrix + third_coef * square
        iterate = first_coef * iterate + jnp.einsum('ij,jl->il', polynomial, iterate, precision=lax.Precision.HIGHEST, preferred_element_type=jnp.float32)
    return 0.2 * math.sqrt(max(BLOCK, D)) * iterate

def reference(gradient, momentum):
    widened = gradient.astype(jnp.float32)
    momentum_out = decay_rate * momentum + widened
    direction = widened + decay_rate * momentum_out
    update = lax.map(orthogonalize, direction)
    return (momentum_out, update)
```

```python
import functools
import math

import jax
import jax.numpy as jnp
from jax import lax
from jax.experimental import pallas as pl
from jax.experimental.pallas import tpu as pltpu
from jax.sharding import PartitionSpec as P

ITERS = 3
TILE = 256

first_coef = 3.4445
second_coef = -4.775
third_coef = 2.0315
decay_rate = 0.95


def halves(value):
    high = value.astype(jnp.bfloat16)
    low = (value - high.astype(jnp.float32)).astype(jnp.bfloat16)
    return high, low


def split_dot(left_pair, right_high, right_low, contract):
    rows, depth = left_pair.shape[1:]
    dims = (((1,), (contract,)), ((), ()))
    both = lax.dot_general(
        left_pair.reshape(2 * rows, depth), right_high, dims, preferred_element_type=jnp.float32
    )
    cross = lax.dot_general(left_pair[0], right_low, dims, preferred_element_type=jnp.float32)
    return both[:rows] + (both[rows:] + cross)


def upper_tile(step, count):
    row = jnp.int32(0)
    offset = jnp.int32(0)
    passed = 0
    for index in range(count - 1):
        passed += count - index
        beyond = (step >= passed).astype(jnp.int32)
        row += beyond
        offset += beyond * (count - index)
    return row, step - offset + row


def columns_of(index):
    return pl.ds(pl.multiple_of(index * TILE, TILE), TILE)


def put_symmetric(out, row, column, value):
    high, low = halves(value)
    out[row, 0, :, columns_of(column)] = high
    out[row, 1, :, columns_of(column)] = low
    high, low = halves(value.T)
    out[column, 0, :, columns_of(row)] = high
    out[column, 1, :, columns_of(row)] = low


def column_halves(matrix, column):
    count = matrix.shape[0]
    depth = count * TILE
    cols = columns_of(column)
    return (
        matrix[:, 0, :, cols].reshape(depth, TILE),
        matrix[:, 1, :, cols].reshape(depth, TILE),
    )


def symmetric_product(out, left, right, finish=None):
    count = left.shape[0]

    def body(step, carry):
        row, column = upper_tile(step, count)
        right_high, right_low = column_halves(right, column)
        value = split_dot(left[row], right_high, right_low, 0)
        if finish is not None:
            value = finish(row, column, value)
        put_symmetric(out, row, column, value)
        return carry

    lax.fori_loop(0, count * (count + 1) // 2, body, 0)


def gram_of(out, matrix):
    count = matrix.shape[0]

    def body(step, carry):
        row, column = upper_tile(step, count)
        value = split_dot(matrix[row], matrix[column, 0], matrix[column, 1], 1)
        put_symmetric(out, row, column, value)
        return carry

    lax.fori_loop(0, count * (count + 1) // 2, body, 0)


def polynomial_of(out, gram):
    def finish(row, column, square):
        cols = columns_of(column)
        tile = gram[row, 0, :, cols].astype(jnp.float32) + gram[row, 1, :, cols].astype(jnp.float32)
        value = second_coef * tile + third_coef * square
        rows_at = lax.broadcasted_iota(jnp.int32, (TILE, TILE), 0) + row * TILE
        cols_at = lax.broadcasted_iota(jnp.int32, (TILE, TILE), 1) + column * TILE
        return value + jnp.where(rows_at == cols_at, first_coef, 0.0)

    symmetric_product(out, gram, gram, finish)


def orthogonalize(own, result, whole, gram, poly, mixed, mine, scale):
    count = whole.shape[0]
    gram_of(gram, whole)
    for index in range(count):
        rows = slice(index * TILE, (index + 1) * TILE)
        high, low = halves(own[rows, :] * scale)
        mine[0, 0, rows, :] = high
        mine[0, 1, rows, :] = low
    for sweep in range(ITERS):
        polynomial_of(poly, gram)
        now, later = sweep % 2, (sweep + 1) % 2
        last = sweep == ITERS - 1

        def body(row, carry):
            value = split_dot(poly[row], mine[now, 0], mine[now, 1], 0)
            rows = pl.ds(pl.multiple_of(row * TILE, TILE), TILE)
            if last:
                result[rows, :] = 0.2 * math.sqrt(count * TILE) * value
            else:
                high, low = halves(value)
                mine[later, 0, rows, :] = high
                mine[later, 1, rows, :] = low
            return carry

        lax.fori_loop(0, count, body, 0)
        if not last:
            symmetric_product(mixed, poly, gram)
            symmetric_product(gram, mixed, poly)


def kernel(pieces, own, result, whole, gram, poly, mixed, mine):
    parts, height, width = pieces.shape
    count = height // TILE
    total = jnp.zeros((8, width), jnp.float32)
    for part in range(parts):
        for index in range(count):
            value = pieces[part, index * TILE : (index + 1) * TILE, :]
            total += jnp.sum((value * value).reshape(TILE // 8, 8, width), axis=0)
    scale = 1.0 / (jnp.sqrt(jnp.sum(total)) + 1e-07)
    for part in range(parts):
        cols = slice(part * width, (part + 1) * width)
        for index in range(count):
            high, low = halves(pieces[part, index * TILE : (index + 1) * TILE, :] * scale)
            whole[index, 0, :, cols] = high
            whole[index, 1, :, cols] = low
    orthogonalize(own, result, whole, gram, poly, mixed, mine, scale)


def per_device(gradient, momentum):
    widened = gradient.astype(jnp.float32)
    momentum_out = decay_rate * momentum + widened
    direction = widened + decay_rate * momentum_out
    blocks, rows, width = direction.shape
    by_owner = lax.all_to_all(direction, "shard", split_axis=0, concat_axis=0, tiled=True)
    own = by_owner.reshape(blocks * rows, width)
    pieces = lax.all_gather(own, "tensor", axis=0)
    height = own.shape[0]
    count = height // TILE
    square = pltpu.VMEM((count, 2, TILE, height), jnp.bfloat16)
    result = pl.pallas_call(
        kernel,
        out_shape=jax.ShapeDtypeStruct((height, width), jnp.float32),
        in_specs=[pl.BlockSpec(memory_space=pltpu.VMEM)] * 2,
        out_specs=pl.BlockSpec(memory_space=pltpu.VMEM),
        scratch_shapes=[
            pltpu.VMEM((count, 2, TILE, pieces.shape[0] * width), jnp.bfloat16),
            square,
            square,
            square,
            pltpu.VMEM((2, 2, height, width), jnp.bfloat16),
        ],
        compiler_params=pltpu.CompilerParams(vmem_limit_bytes=50 * 1024 * 1024),
    )(pieces, own)
    update = lax.all_to_all(
        result.reshape(blocks, rows, width), "shard", split_axis=0, concat_axis=0, tiled=True
    )
    return (momentum_out, update)


def solution(mesh):
    placed = P(None, "shard", "tensor")
    return jax.shard_map(
        per_device,
        mesh=mesh,
        in_specs=(placed, placed),
        out_specs=(placed, placed),
        check_vma=False,
    )
```

```python
import functools
import math

import jax
import jax.numpy as jnp
from jax import lax
from jax.experimental import pallas as pl
from jax.experimental.pallas import tpu as pltpu
from jax.sharding import PartitionSpec as P

ITERS = 3
TILE = 256

first_coef = 3.4445
second_coef = -4.775
third_coef = 2.0315
decay_rate = 0.95


def halves(value):
    high = value.astype(jnp.bfloat16)
    low = (value - high.astype(jnp.float32)).astype(jnp.bfloat16)
    return high, low


def split_dot(left_pair, right_high, right_low, contract):
    rows, depth = left_pair.shape[1:]
    dims = (((1,), (contract,)), ((), ()))
    both = lax.dot_general(
        left_pair.reshape(2 * rows, depth), right_high, dims, preferred_element_type=jnp.float32
    )
    cross = lax.dot_general(left_pair[0], right_low, dims, preferred_element_type=jnp.float32)
    return both[:rows] + (both[rows:] + cross)


def upper_tile(step, count):
    row = jnp.int32(0)
    offset = jnp.int32(0)
    passed = 0
    for index in range(count - 1):
        passed += count - index
        beyond = (step >= passed).astype(jnp.int32)
        row += beyond
        offset += beyond * (count - index)
    return row, step - offset + row


def columns_of(index):
    return pl.ds(pl.multiple_of(index * TILE, TILE), TILE)


def put_symmetric(out, row, column, value):
    high, low = halves(value)
    out[row, 0, :, columns_of(column)] = high
    out[row, 1, :, columns_of(column)] = low
    high, low = halves(value.T)
    out[column, 0, :, columns_of(row)] = high
    out[column, 1, :, columns_of(row)] = low


def column_halves(matrix, column):
    count = matrix.shape[0]
    depth = count * TILE
    cols = columns_of(column)
    return (
        matrix[:, 0, :, cols].reshape(depth, TILE),
        matrix[:, 1, :, cols].reshape(depth, TILE),
    )


def symmetric_product(out, left, right, finish=None):
    count = left.shape[0]

    def body(step, carry):
        row, column = upper_tile(step, count)
        right_high, right_low = column_halves(right, column)
        value = split_dot(left[row], right_high, right_low, 0)
        if finish is not None:
            value = finish(row, column, value)
        put_symmetric(out, row, column, value)
        return carry

    lax.fori_loop(0, count * (count + 1) // 2, body, 0)


def gram_of(out, matrix, factor):
    count = matrix.shape[0]

    def body(step, carry):
        row, column = upper_tile(step, count)
        value = split_dot(matrix[row], matrix[column, 0], matrix[column, 1], 1) * factor
        put_symmetric(out, row, column, value)
        return carry

    lax.fori_loop(0, count * (count + 1) // 2, body, 0)


def polynomial_of(out, gram):
    def finish(row, column, square):
        cols = columns_of(column)
        tile = gram[row, 0, :, cols].astype(jnp.float32) + gram[row, 1, :, cols].astype(jnp.float32)
        value = second_coef * tile + third_coef * square
        rows_at = lax.broadcasted_iota(jnp.int32, (TILE, TILE), 0) + row * TILE
        cols_at = lax.broadcasted_iota(jnp.int32, (TILE, TILE), 1) + column * TILE
        return value + jnp.where(rows_at == cols_at, first_coef, 0.0)

    symmetric_product(out, gram, gram, finish)


def orthogonalize(result, whole, gram, poly, mixed, mine, scale, order, send):
    count = whole.shape[0]
    gram_of(gram, whole, scale * scale)
    for sweep in range(ITERS):
        polynomial_of(poly, gram)
        now, later = sweep % 2, (sweep + 1) % 2
        if sweep < ITERS - 1:

            def body(row, carry):
                value = split_dot(poly[row], mine[now, 0], mine[now, 1], 0)
                high, low = halves(value)
                rows = pl.ds(pl.multiple_of(row * TILE, TILE), TILE)
                mine[later, 0, rows, :] = high
                mine[later, 1, rows, :] = low
                return carry

            lax.fori_loop(0, count, body, 0)
            symmetric_product(mixed, poly, gram)
            symmetric_product(gram, mixed, poly)
        else:
            for row in order:
                value = split_dot(poly[row], mine[now, 0], mine[now, 1], 0)
                rows = pl.ds(pl.multiple_of(row * TILE, TILE), TILE)
                result[rows, :] = (0.2 * math.sqrt(count * TILE) * scale) * value
                send(row)


def step_order(count):
    half = count // 2
    return [0] + [d for k in range(half) for d in (half + k, k) if d > 0]


def kernel(shards, direction, update, pieces, result, whole, gram, poly, mixed, mine, sends, arrivals):
    rows, width = direction.shape[1:]
    height = shards * rows
    count = height // TILE
    each = TILE // rows
    me = lax.axis_index("shard")
    lane = lax.axis_index("tensor")
    order = step_order(shards)

    def remote(src, dst, kind, step, target):
        return pltpu.make_async_remote_copy(
            src_ref=src,
            dst_ref=dst,
            send_sem=sends.at[kind, step],
            recv_sem=arrivals.at[kind, step],
            device_id=target,
            device_id_type=pl.DeviceIdType.MESH,
        )

    barrier = pltpu.get_barrier_semaphore()
    for step in range(1, shards):
        pl.semaphore_signal(
            barrier, inc=1, device_id=(me ^ step, lane), device_id_type=pl.DeviceIdType.MESH
        )
    for flip in (1, 2):
        pl.semaphore_signal(
            barrier, inc=1, device_id=(me, lane ^ flip), device_id_type=pl.DeviceIdType.MESH
        )
    pl.semaphore_wait(barrier, shards + 1)

    def place(step):
        return pl.ds(pl.multiple_of((me ^ step) * rows, rows), rows)

    def mine_rows(step):
        return pl.ds(pl.multiple_of(me * rows, rows), rows)

    scatter = {}
    for step in order[1:]:
        scatter[step] = remote(
            direction.at[me ^ step], pieces.at[lane, mine_rows(step)], 0, step, (me ^ step, lane)
        )
        scatter[step].start()

    total = jnp.zeros((8, width), jnp.float32)

    def take(value, step, part, total):
        source = me ^ step
        block = lax.div(source, each)
        inner = pl.ds(pl.multiple_of(lax.rem(source, each) * rows, rows), rows)
        cols = pl.ds(pl.multiple_of(part * width, width), width)
        high, low = halves(value)
        whole[block, 0, inner, cols] = high
        whole[block, 1, inner, cols] = low
        return total + jnp.sum((value * value).reshape(rows // 8, 8, width), axis=0), high, low

    forward = {}
    for index in range(shards + 2):
        if index < shards:
            step = order[index]
            if step == 0:
                src = direction.at[me]
            else:
                scatter[step].wait_recv()
                src = pieces.at[lane, place(step)]
            for kind in (2, 1):
                forward[kind, step] = remote(
                    src, pieces.at[lane, place(step)], kind, step, (me, lane ^ kind)
                )
                forward[kind, step].start()
            total, high, low = take(src[...], step, lane, total)
            mine[0, 0, place(step), :] = high
            mine[0, 1, place(step), :] = low
        if 1 <= index <= shards:
            step = order[index - 1]
            forward[2, step].wait_recv()
            src = pieces.at[lane ^ 2, place(step)]
            forward[3, step] = remote(src, src, 3, step, (me, lane ^ 1))
            forward[3, step].start()
            total, _, _ = take(src[...], step, lane ^ 2, total)
            forward[1, step].wait_recv()
            total, _, _ = take(pieces[lane ^ 1, place(step), :], step, lane ^ 1, total)
        if index >= 2:
            step = order[index - 2]
            forward[3, step].wait_recv()
            total, _, _ = take(pieces[lane ^ 3, place(step), :], step, lane ^ 3, total)
    scale = 1.0 / (jnp.sqrt(jnp.sum(total)) + 1e-07)

    home = lax.div(me, each)
    back = {}

    def back_copy(step):
        return remote(result.at[place(step)], update.at[me], 4, step, (me ^ step, lane))

    flips = list(range(count // 2, count)) + list(range(count // 2))[::-1]
    sent = iter(flips)

    def send(row):
        flip = next(sent)
        for inner in range(each):
            step = flip * each + inner
            if step == 0:
                update[me] = result[mine_rows(step), :]
            else:
                back[step] = back_copy(step)
                back[step].start()

    orthogonalize(
        result, whole, gram, poly, mixed, mine, scale, [home ^ flip for flip in flips], send
    )
    for step in order[1:]:
        back[step].wait()
    for copy in list(scatter.values()) + list(forward.values()):
        copy.wait_send()


def per_device(shards, gradient, momentum):
    widened = gradient.astype(jnp.float32)
    momentum_out = decay_rate * momentum + widened
    direction = widened + decay_rate * momentum_out
    blocks, rows, width = direction.shape
    height = blocks * rows
    count = height // TILE
    parts = 4
    square = pltpu.VMEM((count, 2, TILE, height), jnp.bfloat16)
    update = pl.pallas_call(
        functools.partial(kernel, shards),
        out_shape=jax.ShapeDtypeStruct((blocks, rows, width), jnp.float32),
        in_specs=[pl.BlockSpec(memory_space=pltpu.VMEM)],
        out_specs=pl.BlockSpec(memory_space=pltpu.VMEM),
        scratch_shapes=[
            pltpu.VMEM((parts, height, width), jnp.float32),
            pltpu.VMEM((height, width), jnp.float32),
            pltpu.VMEM((count, 2, TILE, parts * width), jnp.bfloat16),
            square,
            square,
            square,
            pltpu.VMEM((2, 2, height, width), jnp.bfloat16),
            pltpu.SemaphoreType.DMA((5, shards)),
            pltpu.SemaphoreType.DMA((5, shards)),
        ],
        compiler_params=pltpu.CompilerParams(
            collective_id=0, has_side_effects=True, vmem_limit_bytes=50 * 1024 * 1024
        ),
    )(direction)
    return (momentum_out, update)


def solution(mesh):
    placed = P(None, "shard", "tensor")
    assert mesh.shape["tensor"] == 4
    return jax.shard_map(
        functools.partial(per_device, mesh.shape["shard"]),
        mesh=mesh,
        in_specs=(placed, placed),
        out_specs=(placed, placed),
        check_vma=False,
    )
```

```python
import functools
import math

import jax
import jax.numpy as jnp
from jax import lax
from jax.experimental import pallas as pl
from jax.experimental.pallas import tpu as pltpu
from jax.sharding import PartitionSpec as P

ITERS = 3
TILE = 256

first_coef = 3.4445
second_coef = -4.775
third_coef = 2.0315
decay_rate = 0.95


def halves(value):
    high = value.astype(jnp.bfloat16)
    low = (value - high.astype(jnp.float32)).astype(jnp.bfloat16)
    return high, low


def split_dot(left_pair, right_high, right_low, contract):
    rows, depth = left_pair.shape[1:]
    dims = (((1,), (contract,)), ((), ()))
    both = lax.dot_general(
        left_pair.reshape(2 * rows, depth), right_high, dims, preferred_element_type=jnp.float32
    )
    cross = lax.dot_general(left_pair[0], right_low, dims, preferred_element_type=jnp.float32)
    return both[:rows] + (both[rows:] + cross)


def upper_tiles(count):
    return [(row, column) for column in range(count) for row in range(column + 1)]


def columns_of(index):
    return pl.ds(index * TILE, TILE)


def put_symmetric(out, row, column, value):
    high, low = halves(value)
    out[row, 0, :, columns_of(column)] = high
    out[row, 1, :, columns_of(column)] = low
    if row == column:
        return
    high, low = halves(value.T)
    out[column, 0, :, columns_of(row)] = high
    out[column, 1, :, columns_of(row)] = low


def column_halves(matrix, column):
    count = matrix.shape[0]
    depth = count * TILE
    cols = columns_of(column)
    return (
        matrix[:, 0, :, cols].reshape(depth, TILE),
        matrix[:, 1, :, cols].reshape(depth, TILE),
    )


def symmetric_product(out, left, right, finish=None):
    count = left.shape[0]

    for row, column in upper_tiles(count):
        right_high, right_low = column_halves(right, column)
        value = split_dot(left[row], right_high, right_low, 0)
        if finish is not None:
            value = finish(row, column, value)
        put_symmetric(out, row, column, value)


def gram_of(out, matrix, factor):
    count = matrix.shape[0]

    for row, column in upper_tiles(count):
        value = split_dot(matrix[row], matrix[column, 0], matrix[column, 1], 1) * factor
        put_symmetric(out, row, column, value)


def polynomial_of(out, gram):
    def finish(row, column, square):
        cols = columns_of(column)
        tile = gram[row, 0, :, cols].astype(jnp.float32) + gram[row, 1, :, cols].astype(jnp.float32)
        value = second_coef * tile + third_coef * square
        if row != column:
            return value
        rows_at = lax.broadcasted_iota(jnp.int32, (TILE, TILE), 0)
        cols_at = lax.broadcasted_iota(jnp.int32, (TILE, TILE), 1)
        return value + jnp.where(rows_at == cols_at, first_coef, 0.0)

    symmetric_product(out, gram, gram, finish)


def orthogonalize(result, whole, gram, poly, mixed, mine, scale, order, send):
    count = whole.shape[0]
    gram_of(gram, whole, scale * scale)
    for sweep in range(ITERS):
        polynomial_of(poly, gram)
        now, later = sweep % 2, (sweep + 1) % 2
        if sweep < ITERS - 1:
            for row in range(count):
                value = split_dot(poly[row], mine[now, 0], mine[now, 1], 0)
                high, low = halves(value)
                mine[later, 0, columns_of(row), :] = high
                mine[later, 1, columns_of(row), :] = low
            symmetric_product(mixed, poly, gram)
            symmetric_product(gram, mixed, poly)
        else:
            for row in order:
                value = split_dot(poly[row], mine[now, 0], mine[now, 1], 0)
                rows = pl.ds(pl.multiple_of(row * TILE, TILE), TILE)
                result[rows, :] = (0.2 * math.sqrt(count * TILE) * scale) * value
                send(row)


def step_order(count):
    half = count // 2
    return [0] + [d for k in range(half) for d in (half + k, k) if d > 0]


def kernel(shards, direction, update, pieces, result, whole, gram, poly, mixed, mine, sends, arrivals):
    rows, width = direction.shape[1:]
    height = shards * rows
    count = height // TILE
    each = TILE // rows
    me = lax.axis_index("shard")
    lane = lax.axis_index("tensor")
    order = step_order(shards)

    def remote(src, dst, kind, step, target):
        return pltpu.make_async_remote_copy(
            src_ref=src,
            dst_ref=dst,
            send_sem=sends.at[kind, step],
            recv_sem=arrivals.at[kind, step],
            device_id=target,
            device_id_type=pl.DeviceIdType.MESH,
        )

    barrier = pltpu.get_barrier_semaphore()
    for step in range(1, shards):
        pl.semaphore_signal(
            barrier, inc=1, device_id=(me ^ step, lane), device_id_type=pl.DeviceIdType.MESH
        )
    for flip in (1, 2):
        pl.semaphore_signal(
            barrier, inc=1, device_id=(me, lane ^ flip), device_id_type=pl.DeviceIdType.MESH
        )
    pl.semaphore_wait(barrier, shards + 1)

    def place(step):
        return pl.ds(pl.multiple_of((me ^ step) * rows, rows), rows)

    def mine_rows(step):
        return pl.ds(pl.multiple_of(me * rows, rows), rows)

    scatter = {}
    for step in order[1:]:
        scatter[step] = remote(
            direction.at[me ^ step], pieces.at[lane, mine_rows(step)], 0, step, (me ^ step, lane)
        )
        scatter[step].start()

    total = jnp.zeros((8, width), jnp.float32)

    def take(value, step, part, total):
        source = me ^ step
        block = lax.div(source, each)
        inner = pl.ds(pl.multiple_of(lax.rem(source, each) * rows, rows), rows)
        cols = pl.ds(pl.multiple_of(part * width, width), width)
        high, low = halves(value)
        whole[block, 0, inner, cols] = high
        whole[block, 1, inner, cols] = low
        return total + jnp.sum((value * value).reshape(rows // 8, 8, width), axis=0), high, low

    forward = {}
    for index in range(shards + 2):
        if index < shards:
            step = order[index]
            if step == 0:
                src = direction.at[me]
            else:
                scatter[step].wait_recv()
                src = pieces.at[lane, place(step)]
            for kind in (2, 1):
                forward[kind, step] = remote(
                    src, pieces.at[lane, place(step)], kind, step, (me, lane ^ kind)
                )
                forward[kind, step].start()
            total, high, low = take(src[...], step, lane, total)
            mine[0, 0, place(step), :] = high
            mine[0, 1, place(step), :] = low
        if 1 <= index <= shards:
            step = order[index - 1]
            forward[2, step].wait_recv()
            src = pieces.at[lane ^ 2, place(step)]
            forward[3, step] = remote(src, src, 3, step, (me, lane ^ 1))
            forward[3, step].start()
            total, _, _ = take(src[...], step, lane ^ 2, total)
            forward[1, step].wait_recv()
            total, _, _ = take(pieces[lane ^ 1, place(step), :], step, lane ^ 1, total)
        if index >= 2:
            step = order[index - 2]
            forward[3, step].wait_recv()
            total, _, _ = take(pieces[lane ^ 3, place(step), :], step, lane ^ 3, total)
    scale = 1.0 / (jnp.sqrt(jnp.sum(total)) + 1e-07)

    home = lax.div(me, each)
    back = {}

    def back_copy(step):
        return remote(result.at[place(step)], update.at[me], 4, step, (me ^ step, lane))

    flips = list(range(count // 2, count)) + list(range(count // 2))[::-1]
    sent = iter(flips)

    def send(row):
        flip = next(sent)
        for inner in range(each):
            step = flip * each + inner
            if step == 0:
                update[me] = result[mine_rows(step), :]
            else:
                back[step] = back_copy(step)
                back[step].start()

    orthogonalize(
        result, whole, gram, poly, mixed, mine, scale, [home ^ flip for flip in flips], send
    )
    for step in order[1:]:
        back[step].wait()
    for copy in list(scatter.values()) + list(forward.values()):
        copy.wait_send()


def per_device(shards, gradient, momentum):
    widened = gradient.astype(jnp.float32)
    momentum_out = decay_rate * momentum + widened
    direction = widened + decay_rate * momentum_out
    blocks, rows, width = direction.shape
    height = blocks * rows
    count = height // TILE
    parts = 4
    square = pltpu.VMEM((count, 2, TILE, height), jnp.bfloat16)
    update = pl.pallas_call(
        functools.partial(kernel, shards),
        out_shape=jax.ShapeDtypeStruct((blocks, rows, width), jnp.float32),
        in_specs=[pl.BlockSpec(memory_space=pltpu.VMEM)],
        out_specs=pl.BlockSpec(memory_space=pltpu.VMEM),
        scratch_shapes=[
            pltpu.VMEM((parts, height, width), jnp.float32),
            pltpu.VMEM((height, width), jnp.float32),
            pltpu.VMEM((count, 2, TILE, parts * width), jnp.bfloat16),
            square,
            square,
            square,
            pltpu.VMEM((2, 2, height, width), jnp.bfloat16),
            pltpu.SemaphoreType.DMA((5, shards)),
            pltpu.SemaphoreType.DMA((5, shards)),
        ],
        compiler_params=pltpu.CompilerParams(
            collective_id=0, has_side_effects=True, vmem_limit_bytes=50 * 1024 * 1024
        ),
    )(direction)
    return (momentum_out, update)


def solution(mesh):
    placed = P(None, "shard", "tensor")
    assert mesh.shape["tensor"] == 4
    return jax.shard_map(
        functools.partial(per_device, mesh.shape["shard"]),
        mesh=mesh,
        in_specs=(placed, placed),
        out_specs=(placed, placed),
        check_vma=False,
    )
```

```python
import functools
import math

import jax
import jax.numpy as jnp
from jax import lax
from jax.experimental import pallas as pl
from jax.experimental.pallas import tpu as pltpu
from jax.sharding import PartitionSpec as P

ITERS = 3
TILE = 256

first_coef = 3.4445
second_coef = -4.775
third_coef = 2.0315
decay_rate = 0.95


def halves(value):
    high = value.astype(jnp.bfloat16)
    low = (value - high.astype(jnp.float32)).astype(jnp.bfloat16)
    return high, low


def split_dot(left_pair, right_high, right_low, contract):
    rows, depth = left_pair.shape[1:]
    dims = (((1,), (contract,)), ((), ()))
    both = lax.dot_general(
        left_pair.reshape(2 * rows, depth), right_high, dims, preferred_element_type=jnp.float32
    )
    cross = lax.dot_general(left_pair[0], right_low, dims, preferred_element_type=jnp.float32)
    return both[:rows] + (both[rows:] + cross)


def upper_tiles(count):
    return [(row, column) for column in range(count) for row in range(column + 1)]


def columns_of(index):
    return pl.ds(index * TILE, TILE)


def put_symmetric(out, row, column, value):
    high, low = halves(value)
    out[row, 0, :, columns_of(column)] = high
    out[row, 1, :, columns_of(column)] = low
    if row == column:
        return
    high, low = halves(value.T)
    out[column, 0, :, columns_of(row)] = high
    out[column, 1, :, columns_of(row)] = low


def column_halves(matrix, column):
    count = matrix.shape[0]
    depth = count * TILE
    cols = columns_of(column)
    return (
        matrix[:, 0, :, cols].reshape(depth, TILE),
        matrix[:, 1, :, cols].reshape(depth, TILE),
    )


def symmetric_product(out, left, right, finish=None):
    count = left.shape[0]

    for row, column in upper_tiles(count):
        right_high, right_low = column_halves(right, column)
        value = split_dot(left[row], right_high, right_low, 0)
        if finish is not None:
            value = finish(row, column, value)
        put_symmetric(out, row, column, value)


def gram_tile(matrix, row, column):
    return split_dot(matrix[row], matrix[column, 0], matrix[column, 1], 1)


def polynomial_of(out, gram):
    def finish(row, column, square):
        cols = columns_of(column)
        tile = gram[row, 0, :, cols].astype(jnp.float32) + gram[row, 1, :, cols].astype(jnp.float32)
        value = second_coef * tile + third_coef * square
        if row != column:
            return value
        rows_at = lax.broadcasted_iota(jnp.int32, (TILE, TILE), 0)
        cols_at = lax.broadcasted_iota(jnp.int32, (TILE, TILE), 1)
        return value + jnp.where(rows_at == cols_at, first_coef, 0.0)

    symmetric_product(out, gram, gram, finish)


def joined(mine, slot, row):
    rows = columns_of(row)
    return mine[slot, 0, rows, :].astype(jnp.float32) + mine[slot, 1, rows, :].astype(jnp.float32)


def put_rows(mine, slot, row, value):
    high, low = halves(value)
    mine[slot, 0, columns_of(row), :] = high
    mine[slot, 1, columns_of(row), :] = low


def orthogonalize(result, gram, poly, mixed, mine, scale, order, send):
    count = gram.shape[0]
    for sweep in range(ITERS - 1):
        polynomial_of(poly, gram)
        now, later = sweep % 2, (sweep + 1) % 2
        for row in range(count):
            put_rows(mine, later, row, split_dot(poly[row], mine[now, 0], mine[now, 1], 0))
        symmetric_product(mixed, poly, gram)
        symmetric_product(gram, mixed, poly)
    now, later = (ITERS - 1) % 2, ITERS % 2
    for row in range(count):
        value = split_dot(gram[row], mine[now, 0], mine[now, 1], 0)
        put_rows(mine, later, row, second_coef * joined(mine, now, row) + third_coef * value)
    for row in order:
        value = split_dot(gram[row], mine[later, 0], mine[later, 1], 0)
        value = first_coef * joined(mine, now, row) + value
        result[columns_of(row), :] = (0.2 * math.sqrt(count * TILE) * scale) * value
        send(row)


def block_order(count):
    half = count // 2
    return [block for k in range(half) for block in (k, half + k)]


def kernel(shards, direction, update, pieces, result, whole, gram, poly, mixed, mine, tiles, sends, arrivals):
    rows, width = direction.shape[1:]
    height = shards * rows
    count = height // TILE
    each = TILE // rows
    me = lax.axis_index("shard")
    lane = lax.axis_index("tensor")
    blocks = block_order(count)
    order = [block * each + inner for block in blocks for inner in range(each)]

    def remote(src, dst, kind, step, target):
        return pltpu.make_async_remote_copy(
            src_ref=src,
            dst_ref=dst,
            send_sem=sends.at[kind, step],
            recv_sem=arrivals.at[kind, step],
            device_id=target,
            device_id_type=pl.DeviceIdType.MESH,
        )

    barrier = pltpu.get_barrier_semaphore()
    for step in range(1, shards):
        pl.semaphore_signal(
            barrier, inc=1, device_id=(me ^ step, lane), device_id_type=pl.DeviceIdType.MESH
        )
    for flip in (1, 2):
        pl.semaphore_signal(
            barrier, inc=1, device_id=(me, lane ^ flip), device_id_type=pl.DeviceIdType.MESH
        )
    pl.semaphore_wait(barrier, shards + 1)

    def place(step):
        return pl.ds(step * rows, rows)

    scatter = {}
    for step in order[1:]:
        scatter[step] = remote(
            direction.at[me ^ step], pieces.at[lane, place(step)], 0, step, (me ^ step, lane)
        )
        scatter[step].start()

    total = jnp.zeros((8, width), jnp.float32)

    def take(value, step, part, total):
        block = step // each
        inner = pl.ds(step % each * rows, rows)
        cols = pl.ds(part * width, width)
        high, low = halves(value)
        whole[block, 0, inner, cols] = high
        whole[block, 1, inner, cols] = low
        return total + jnp.sum((value * value).reshape(rows // 8, 8, width), axis=0), high, low

    forward = {}
    placed = []
    for index in range(shards + 2):
        if index < shards:
            step = order[index]
            if step == 0:
                src = direction.at[me]
            else:
                scatter[step].wait_recv()
                src = pieces.at[lane, place(step)]
            for kind in (2, 1):
                forward[kind, step] = remote(
                    src, pieces.at[lane, place(step)], kind, step, (me, lane ^ kind)
                )
                forward[kind, step].start()
            total, high, low = take(src[...], step, 0, total)
            mine[0, 0, place(step), :] = high
            mine[0, 1, place(step), :] = low
        if 1 <= index <= shards:
            step = order[index - 1]
            forward[2, step].wait_recv()
            src = pieces.at[lane ^ 2, place(step)]
            forward[3, step] = remote(src, src, 3, step, (me, lane ^ 1))
            forward[3, step].start()
            total, _, _ = take(src[...], step, 2, total)
            forward[1, step].wait_recv()
            total, _, _ = take(pieces[lane ^ 1, place(step), :], step, 1, total)
        if index >= 2:
            step = order[index - 2]
            forward[3, step].wait_recv()
            total, _, _ = take(pieces[lane ^ 3, place(step), :], step, 3, total)
            complete = (index - 1) // each
            if (index - 1) % each == 0 and complete < count:
                row = blocks[complete - 1]
                for column in blocks[:complete]:
                    tiles[len(placed)] = gram_tile(whole, row, column)
                    placed.append((row, column))
    scale = 1.0 / (jnp.sqrt(jnp.sum(total)) + 1e-07)

    for slot, (row, column) in enumerate(placed):
        put_symmetric(gram, row, column, tiles[slot] * (scale * scale))
    for column in blocks:
        value = gram_tile(whole, blocks[-1], column) * (scale * scale)
        put_symmetric(gram, blocks[-1], column, value)

    back = {}

    def back_copy(step):
        return remote(result.at[place(step)], update.at[me], 4, step, (me ^ step, lane))

    def send(row):
        for inner in range(each):
            step = row * each + inner
            if step == 0:
                update[me] = result[place(step), :]
            else:
                back[step] = back_copy(step)
                back[step].start()

    farthest = list(range(count // 2, count)) + list(range(count // 2))[::-1]
    orthogonalize(result, gram, poly, mixed, mine, scale, farthest, send)
    for step in order[1:]:
        back[step].wait()
    for copy in list(scatter.values()) + list(forward.values()):
        copy.wait_send()


def per_device(shards, gradient, momentum):
    widened = gradient.astype(jnp.float32)
    momentum_out = decay_rate * momentum + widened
    direction = widened + decay_rate * momentum_out
    blocks, rows, width = direction.shape
    height = blocks * rows
    count = height // TILE
    parts = 4
    square = pltpu.VMEM((count, 2, TILE, height), jnp.bfloat16)
    update = pl.pallas_call(
        functools.partial(kernel, shards),
        out_shape=jax.ShapeDtypeStruct((blocks, rows, width), jnp.float32),
        in_specs=[pl.BlockSpec(memory_space=pltpu.VMEM)],
        out_specs=pl.BlockSpec(memory_space=pltpu.VMEM),
        scratch_shapes=[
            pltpu.VMEM((parts, height, width), jnp.float32),
            pltpu.VMEM((height, width), jnp.float32),
            pltpu.VMEM((count, 2, TILE, parts * width), jnp.bfloat16),
            square,
            square,
            square,
            pltpu.VMEM((2, 2, height, width), jnp.bfloat16),
            pltpu.VMEM((count * (count - 1) // 2, TILE, TILE), jnp.float32),
            pltpu.SemaphoreType.DMA((5, shards)),
            pltpu.SemaphoreType.DMA((5, shards)),
        ],
        compiler_params=pltpu.CompilerParams(
            collective_id=0, has_side_effects=True, vmem_limit_bytes=50 * 1024 * 1024
        ),
    )(direction)
    return (momentum_out, update)


def solution(mesh):
    placed = P(None, "shard", "tensor")
    assert mesh.shape["tensor"] == 4
    return jax.shard_map(
        functools.partial(per_device, mesh.shape["shard"]),
        mesh=mesh,
        in_specs=(placed, placed),
        out_specs=(placed, placed),
        check_vma=False,
    )
```

```python
import functools
import math

import jax
import jax.numpy as jnp
from jax import lax
from jax.experimental import pallas as pl
from jax.experimental.pallas import tpu as pltpu
from jax.sharding import PartitionSpec as P

ITERS = 3
TILE = 256

first_coef = 3.4445
second_coef = -4.775
third_coef = 2.0315
decay_rate = 0.95


def halves(value):
    high = value.astype(jnp.bfloat16)
    low = (value - high.astype(jnp.float32)).astype(jnp.bfloat16)
    return high, low


def split_dot(left_pair, right_high, right_low, contract):
    rows, depth = left_pair.shape[1:]
    dims = (((1,), (contract,)), ((), ()))
    both = lax.dot_general(
        left_pair.reshape(2 * rows, depth), right_high, dims, preferred_element_type=jnp.float32
    )
    cross = lax.dot_general(left_pair[0], right_low, dims, preferred_element_type=jnp.float32)
    return both[:rows] + (both[rows:] + cross)


def upper_tiles(count):
    return [(row, column) for column in range(count) for row in range(column + 1)]


def columns_of(index):
    return pl.ds(index * TILE, TILE)


def put_symmetric(out, row, column, value):
    high, low = halves(value)
    out[row, 0, :, columns_of(column)] = high
    out[row, 1, :, columns_of(column)] = low
    if row == column:
        return
    high, low = halves(value.T)
    out[column, 0, :, columns_of(row)] = high
    out[column, 1, :, columns_of(row)] = low


def column_halves(matrix, column):
    count = matrix.shape[0]
    depth = count * TILE
    cols = columns_of(column)
    return (
        matrix[:, 0, :, cols].reshape(depth, TILE),
        matrix[:, 1, :, cols].reshape(depth, TILE),
    )


def symmetric_product(out, left, right, finish=None):
    count = left.shape[0]

    for row, column in upper_tiles(count):
        right_high, right_low = column_halves(right, column)
        value = split_dot(left[row], right_high, right_low, 0)
        if finish is not None:
            value = finish(row, column, value)
        put_symmetric(out, row, column, value)


def gram_tile(matrix, row, column):
    return split_dot(matrix[row], matrix[column, 0], matrix[column, 1], 1)


def polynomial_of(out, gram):
    def finish(row, column, square):
        cols = columns_of(column)
        tile = gram[row, 0, :, cols].astype(jnp.float32) + gram[row, 1, :, cols].astype(jnp.float32)
        value = second_coef * tile + third_coef * square
        if row != column:
            return value
        rows_at = lax.broadcasted_iota(jnp.int32, (TILE, TILE), 0)
        cols_at = lax.broadcasted_iota(jnp.int32, (TILE, TILE), 1)
        return value + jnp.where(rows_at == cols_at, first_coef, 0.0)

    symmetric_product(out, gram, gram, finish)


def joined(mine, slot, row):
    rows = columns_of(row)
    return mine[slot, 0, rows, :].astype(jnp.float32) + mine[slot, 1, rows, :].astype(jnp.float32)


def put_rows(mine, slot, row, value):
    high, low = halves(value)
    mine[slot, 0, columns_of(row), :] = high
    mine[slot, 1, columns_of(row), :] = low


def orthogonalize(result, gram, poly, mixed, mine, scale, order, send):
    count = gram.shape[0]
    for sweep in range(ITERS - 1):
        polynomial_of(poly, gram)
        now, later = sweep % 2, (sweep + 1) % 2
        for row in range(count):
            put_rows(mine, later, row, split_dot(poly[row], mine[now, 0], mine[now, 1], 0))
        symmetric_product(mixed, poly, gram)
        symmetric_product(gram, mixed, poly)
    now, later = (ITERS - 1) % 2, ITERS % 2
    for row in range(count):
        value = split_dot(gram[row], mine[now, 0], mine[now, 1], 0)
        put_rows(mine, later, row, second_coef * joined(mine, now, row) + third_coef * value)
    for row in order:
        value = split_dot(gram[row], mine[later, 0], mine[later, 1], 0)
        value = first_coef * joined(mine, now, row) + value
        result[columns_of(row), :] = (0.2 * math.sqrt(count * TILE) * scale) * value
        send(row)


def block_order(count):
    half = count // 2
    return [block for k in range(half) for block in (k, half + k)]


def kernel(shards, direction, update, pieces, result, whole, gram, poly, mixed, mine, tiles, sends, arrivals):
    rows, width = direction.shape[1:]
    height = shards * rows
    count = height // TILE
    each = TILE // rows
    me = lax.axis_index("shard")
    lane = lax.axis_index("tensor")
    blocks = block_order(count)
    order = [block * each + inner for block in blocks for inner in range(each)]

    def remote(src, dst, kind, step, target):
        return pltpu.make_async_remote_copy(
            src_ref=src,
            dst_ref=dst,
            send_sem=sends.at[kind, step],
            recv_sem=arrivals.at[kind, step],
            device_id=target,
            device_id_type=pl.DeviceIdType.MESH,
        )

    barrier = pltpu.get_barrier_semaphore()
    for step in range(1, shards):
        pl.semaphore_signal(
            barrier, inc=1, device_id=(me ^ step, lane), device_id_type=pl.DeviceIdType.MESH
        )
    for flip in (1, 2):
        pl.semaphore_signal(
            barrier, inc=1, device_id=(me, lane ^ flip), device_id_type=pl.DeviceIdType.MESH
        )
    pl.semaphore_wait(barrier, shards + 1)

    def place(step):
        return pl.ds(step * rows, rows)

    scatter = {}
    for step in order[1:]:
        scatter[step] = remote(
            direction.at[me ^ step], pieces.at[lane, place(step)], 0, step, (me ^ step, lane)
        )

    follows = dict(zip(order[each : 2 * each], order[-each:]))
    for step in order[1:-each]:
        scatter[step].start()

    total = jnp.zeros((8, width), jnp.float32)

    def take(value, step, part, total):
        block = step // each
        inner = pl.ds(step % each * rows, rows)
        cols = pl.ds(part * width, width)
        high, low = halves(value)
        whole[block, 0, inner, cols] = high
        whole[block, 1, inner, cols] = low
        return total + jnp.sum((value * value).reshape(rows // 8, 8, width), axis=0), high, low

    forward = {}
    placed = []
    for index in range(shards + 2):
        if index < shards:
            step = order[index]
            if step == 0:
                src = direction.at[me]
            else:
                if step in follows:
                    scatter[step].wait_send()
                    scatter[follows[step]].start()
                scatter[step].wait_recv()
                src = pieces.at[lane, place(step)]
            for kind in (2, 1):
                forward[kind, step] = remote(
                    src, pieces.at[lane, place(step)], kind, step, (me, lane ^ kind)
                )
                forward[kind, step].start()
            total, high, low = take(src[...], step, 0, total)
            mine[0, 0, place(step), :] = high
            mine[0, 1, place(step), :] = low
        if 1 <= index <= shards:
            step = order[index - 1]
            forward[2, step].wait_recv()
            src = pieces.at[lane ^ 2, place(step)]
            forward[3, step] = remote(src, src, 3, step, (me, lane ^ 1))
            forward[3, step].start()
            total, _, _ = take(src[...], step, 2, total)
            forward[1, step].wait_recv()
            total, _, _ = take(pieces[lane ^ 1, place(step), :], step, 1, total)
        if index >= 2:
            step = order[index - 2]
            forward[3, step].wait_recv()
            total, _, _ = take(pieces[lane ^ 3, place(step), :], step, 3, total)
            complete = (index - 1) // each
            if (index - 1) % each == 0 and complete < count:
                row = blocks[complete - 1]
                for column in blocks[:complete]:
                    tiles[len(placed)] = gram_tile(whole, row, column)
                    placed.append((row, column))
    scale = 1.0 / (jnp.sqrt(jnp.sum(total)) + 1e-07)

    for slot, (row, column) in enumerate(placed):
        put_symmetric(gram, row, column, tiles[slot] * (scale * scale))
    for column in blocks:
        value = gram_tile(whole, blocks[-1], column) * (scale * scale)
        put_symmetric(gram, blocks[-1], column, value)

    back = {}

    def back_copy(step):
        return remote(result.at[place(step)], update.at[me], 4, step, (me ^ step, lane))

    def send(row):
        for inner in range(each):
            step = row * each + inner
            if step == 0:
                update[me] = result[place(step), :]
            else:
                back[step] = back_copy(step)
                back[step].start()

    farthest = list(range(count // 2, count)) + list(range(count // 2))[::-1]
    orthogonalize(result, gram, poly, mixed, mine, scale, farthest, send)
    for step in order[1:]:
        back[step].wait()
    for step in order[1:]:
        if step not in follows:
            scatter[step].wait_send()
    for copy in forward.values():
        copy.wait_send()


def per_device(shards, gradient, momentum):
    widened = gradient.astype(jnp.float32)
    momentum_out = decay_rate * momentum + widened
    direction = widened + decay_rate * momentum_out
    blocks, rows, width = direction.shape
    height = blocks * rows
    count = height // TILE
    parts = 4
    square = pltpu.VMEM((count, 2, TILE, height), jnp.bfloat16)
    update = pl.pallas_call(
        functools.partial(kernel, shards),
        out_shape=jax.ShapeDtypeStruct((blocks, rows, width), jnp.float32),
        in_specs=[pl.BlockSpec(memory_space=pltpu.VMEM)],
        out_specs=pl.BlockSpec(memory_space=pltpu.VMEM),
        scratch_shapes=[
            pltpu.VMEM((parts, height, width), jnp.float32),
            pltpu.VMEM((height, width), jnp.float32),
            pltpu.VMEM((count, 2, TILE, parts * width), jnp.bfloat16),
            square,
            square,
            square,
            pltpu.VMEM((2, 2, height, width), jnp.bfloat16),
            pltpu.VMEM((count * (count - 1) // 2, TILE, TILE), jnp.float32),
            pltpu.SemaphoreType.DMA((5, shards)),
            pltpu.SemaphoreType.DMA((5, shards)),
        ],
        compiler_params=pltpu.CompilerParams(
            collective_id=0, has_side_effects=True, vmem_limit_bytes=50 * 1024 * 1024
        ),
    )(direction)
    return (momentum_out, update)


def solution(mesh):
    placed = P(None, "shard", "tensor")
    assert mesh.shape["tensor"] == 4
    return jax.shard_map(
        functools.partial(per_device, mesh.shape["shard"]),
        mesh=mesh,
        in_specs=(placed, placed),
        out_specs=(placed, placed),
        check_vma=False,
    )
```
